32 devices in a mesh: row: 4 (over z), sector: 8 (over y, x, core).
Axes of the slice: x: 2, y: 2, z: 4, core: 2. Of those that a mesh axis runs over, the one named last changes fastest.
Arguments:
- boundary_in: float32 [8, 128, 256], P('sector'), may hold values from -6 to 6
- left_transfer: float32 [4, 8, 128, 128], P('row', 'sector'), may hold values from -0.25 to 0.25
- right_transfer: float32 [4, 256, 256], P('row'), may hold values from -0.36 to 0.36
- env_weight: bfloat16 [4, 4, 256, 256], P('row'), may hold values from -50000 to 50000
- ranks: int32 [8], P('sector'), may hold values from 32 to 128, as said below
- routes: int32 [8, 4], P('sector'), may hold values from 0 to 7, all different within a row; in each aligned block of 8 rows (0 to 7, 8 to 15, ...) at most 6 rows name the same one
- owner: int32 [8], replicated, may hold values from 0 to 7, each once
Outputs:
- boundary_out: float32 [4, 8, 128, 256], P('row', 'sector')
- environment: float32 [4, 8, 128, 256], P('row', 'sector')
The draws below stay inside these ranges and needn't reach their ends.
Inputs may be any that keep to these rules, and one draw needn't show every extreme that they name: `ranks`: at least one sector has rank 128. `routes`: each row names 4 different sectors; no sector is named by more than 6 rows. `owner`: each sector index once.
All inputs are finite; a program needn't handle non-finite values.
Results may differ from the reference program's by a relative error of at most 0.013.
Values may be sent and summed in bfloat16 or wider, within the bound.
A program may use at most 64 MiB of HBM per device.

```python
import math
import jax
import jax.numpy as jnp
import numpy as np
from jax import lax

PAD = 128
D2 = 256
SLOTS = 4
CAP = 6
SECTORS = 8
ROWS = 4


def draw_ranks(key, part):
    values = jax.random.randint(key, (SECTORS,), PAD // 4, PAD + 1)
    position = jax.random.randint(jax.random.fold_in(key, 7), (), 0, SECTORS)
    return jnp.where(jnp.arange(SECTORS) == position, PAD, values).astype(jnp.int32)


def draw_boundary_in(key, part):
    values = jax.random.truncated_normal(key, -6.0, 6.0, (SECTORS, PAD, D2), jnp.float32)
    return values.astype(jnp.float32)


def draw_right_transfer(key, part):
    sigma = 0.5 / jnp.sqrt(jnp.float32(D2))
    values = jax.random.truncated_normal(key, -4.0, 4.0, (ROWS, D2, D2), jnp.float32) * sigma
    values = jnp.clip(values, -0.36, 0.36)
    return values.astype(jnp.float32)


def draw_env_weight(key, part):
    values = jax.random.truncated_normal(key, -4.0, 4.0, (ROWS, SLOTS, D2, D2), jnp.float32)
    values = values / jnp.sqrt(jnp.float32(D2))
    return values.astype(jnp.bfloat16)


def levels(own_key, extent, cuts, least, top_value):
    factor_of, own = 1.0, jax.random.fold_in(own_key, 6)
    for dim, parts in cuts:
        heights = jnp.exp(jax.random.uniform(jax.random.fold_in(own, dim), (parts,), jnp.float32, least / len(cuts), top_value / len(cuts)))
        factor_of = factor_of * jnp.repeat(heights, extent[dim] // parts).reshape([-1 if axis == dim else 1 for axis in range(len(extent))])
    return factor_of


def shared_out(stream_key, own, number, rows, amount, top, most, lean):
    order = jax.random.permutation(stream_key, amount)
    packed, usual = load_shares(amount, rows * top, most, lean, True), load_shares(amount, rows * top, most, lean, False)
    places = jnp.arange(amount)

    def named(sizes, offset_by):
        used = int((sizes > 0).sum())
        fixed = max(1, used // 4)
        shifted = fixed + (places - fixed + offset_by * (used - fixed)) % max(1, amount - fixed)
        return jnp.zeros((amount,), jnp.int32).at[order[jnp.where(places < fixed, places, shifted)]].set(jnp.asarray(sizes, jnp.int32))

    sizes = jnp.where(number % 4 == 0, named(packed, number // 4), named(usual, number - number // 4 - 1))
    mixed = jax.random.permutation(jax.random.fold_in(own, 3), amount)
    source_of, taker = mixed[0:amount // 2 * 2:2], mixed[1:amount // 2 * 2:2]
    slack = jnp.minimum(sizes[source_of] - 1, most - sizes[taker]) // 2
    slack = jnp.where((source_of == order[0]) | (taker == order[0]) | (sizes[taker] == 0), 0, jnp.maximum(slack, 0))
    shifted = jax.random.randint(jax.random.fold_in(own, 4), (amount // 2,), 0, 1 << 20) % (slack + 1)
    sizes = sizes.at[source_of].add(-shifted).at[taker].add(shifted)
    labels = jnp.searchsorted(jnp.cumsum(sizes), jnp.arange(rows * top), side="right").astype(jnp.int32)
    listing = labels.reshape(top, rows).T
    listing = listing[jax.random.permutation(jax.random.fold_in(own, 1), rows)]
    offset_by = jax.random.randint(jax.random.fold_in(own, 2), (rows, 1), 0, top)
    return jnp.take_along_axis(listing, (jnp.arange(top)[None, :] + offset_by) % top, axis=1)


def load_shares(number_of, total, limit, slope, full):
    loads = [(1 << 20) // math.isqrt(standing ** slope) + 1 for standing in range(1, number_of + 1)]
    largest = limit if full else min(limit, max(-(-total // number_of), total * loads[0] // sum(loads)))
    least = 1 if total - largest >= number_of - 1 else 0
    counts, rest = [largest] + [least] * (number_of - 1), total - largest - least * (number_of - 1)
    while rest > 0:
        free = [i for i in range(1, number_of) if counts[i] < largest] or [i for i in range(1, number_of) if counts[i] < limit]
        whole, left = sum([loads[i] for i in free]), rest
        for i in free:
            more = min(limit - counts[i], max(1, left * loads[i] // whole), rest)
            counts[i] = counts[i] + more
            rest = rest - more
    return np.array(counts)


def centred(stream_key, shape, width, bound, pieces=(), kind=jnp.bfloat16):
    result = jax.random.normal(stream_key, shape, jnp.float32) * width
    if len(pieces) > 0:
        result = levels(stream_key, shape, pieces, -0.22, 0.18) * result
    return jnp.clip(result, min=-bound, max=bound).astype(kind)


def setup_inputs(seed: int = 0) -> dict:
    streams_of = jax.random.split(jax.random.key(seed), 8)
    boundary_in = draw_boundary_in(jax.random.fold_in(streams_of[7], 71), 0)
    left_transfer = centred(streams_of[1], (ROWS, SECTORS, PAD, PAD), (4 * PAD) ** -0.5, 0.25, ((0, 4), (1, 8)), jnp.float32)
    right_transfer = draw_right_transfer(jax.random.fold_in(streams_of[7], 71), 0)
    env_weight = draw_env_weight(jax.random.fold_in(streams_of[7], 71), 0)
    ranks = draw_ranks(jax.random.fold_in(streams_of[7], 71), 0)
    routes_keys = jax.random.split(jax.random.fold_in(streams_of[5], 1), SECTORS // SECTORS)
    routes_turns = jax.random.permutation(jax.random.fold_in(streams_of[5], 3), SECTORS // SECTORS)
    routes = jax.vmap(lambda own, number: shared_out(jax.random.fold_in(streams_of[5], 2), own, number, SECTORS, SECTORS, SLOTS, CAP, 2))(routes_keys, routes_turns).reshape((SECTORS, SLOTS))
    owner = jax.random.permutation(streams_of[6], SECTORS).astype(jnp.int32)
    return {"boundary_in": boundary_in, "left_transfer": left_transfer, "right_transfer": right_transfer, "env_weight": env_weight, "ranks": ranks, "routes": routes, "owner": owner}


def reference(boundary_in, left_transfer, right_transfer, env_weight, ranks, routes, owner):
    highest = lax.Precision.HIGHEST
    kept = (jnp.arange(PAD)[None, :] < ranks[:, None]).astype(jnp.float32)
    current = boundary_in * kept[:, :, None]
    unit_block = jnp.eye(PAD, dtype=jnp.float32)
    unit_pairs = jnp.eye(D2, dtype=jnp.float32)
    matches = (routes[:, :, None] == jnp.arange(SECTORS)[None, None, :]).astype(jnp.int32)
    target_owner = jnp.sum(matches * owner[None, None, :], axis=2)
    selector = (target_owner[:, :, None] == jnp.arange(SECTORS)[None, None, :]).astype(jnp.float32)
    bounds = []
    environs = []
    for row_index in range(ROWS):
        left_op = kept[:, :, None] * (0.9 * unit_block + left_transfer[row_index]) * kept[:, None, :]
        right_op = 0.9 * unit_pairs + right_transfer[row_index]
        current = jnp.einsum("sab,sbc->sac", left_op, current, precision=highest)
        current = jnp.einsum("sac,cd->sad", current, right_op, precision=highest)
        bounds.append(current)
        rounded = current.astype(jnp.bfloat16).astype(jnp.float32)
        partials = jnp.einsum("sab,jbc->sjac", rounded, env_weight[row_index].astype(jnp.float32), precision=highest)
        partials = partials.astype(jnp.bfloat16).astype(jnp.float32)
        environs.append(jnp.einsum("sjo,sjac->oac", selector, partials, precision=highest))
    return jnp.stack(bounds), jnp.stack(environs)
```

```python
import functools

import jax
import jax.numpy as jnp
from jax import lax
from jax.experimental import pallas as pl
from jax.experimental.pallas import tpu as pltpu
from jax.sharding import PartitionSpec as P

MESH = pl.DeviceIdType.MESH
BF16 = jnp.bfloat16
F32 = jnp.float32


def partner(index, step, count):
    if count & (count - 1):
        return lax.rem(index + step, count), lax.rem(index - step + count, count)
    result, bit = 0, 1
    while bit < count:
        own = lax.rem(index // bit, 2)
        result = result + ((1 - own) if step & bit else own) * bit
        bit *= 2
    return result, result


def kernel(
    rows, sectors, slices,
    ranks, routes, owner, boundary_in, left, right, weight,
    bound_out, env_out,
    left_bf, left_in, right_bf, y_f32, chain_in, pairs, ys, info, chosen,
    left_send, left_recv, chain_send, chain_recv, pair_send, pair_recv,
    y_send, y_recv, twin_send, info_send, info_recv,
):
    row, sector = lax.axis_index("row"), lax.axis_index("sector")
    slots = weight.shape[1]
    block, width = boundary_in.shape[1], boundary_in.shape[2]
    piece_rows = width // slices
    piece = lax.rem(sector, slices)
    group_base = sector - piece
    groups = sectors // 2
    group, core = sector // 2, lax.rem(sector, 2)
    twin = group * 2 + 1 - core

    barrier = pltpu.get_barrier_semaphore()
    for step in range(1, rows):
        pl.semaphore_signal(barrier, inc=1, device_id=(lax.rem(row + step, rows), sector), device_id_type=MESH)
    for step in range(1, sectors):
        pl.semaphore_signal(barrier, inc=1, device_id=(row, lax.rem(sector + step, sectors)), device_id_type=MESH)

    left_bf[...] = left[0, 0].astype(BF16)
    right_bf[...] = right[0].astype(BF16)
    for j in range(slots):
        info[sector, pl.ds(j, 1), :] = jnp.full((1, 128), owner[routes[0, j]], jnp.int32).astype(F32)
    kept = lax.broadcasted_iota(jnp.int32, (block, width), 0) < ranks[0]

    @pl.when(row == 0)
    def _():
        at = lax.broadcasted_iota(jnp.int32, (piece_rows, width), 0) + piece * piece_rows
        unit = at == lax.broadcasted_iota(jnp.int32, (piece_rows, width), 1)
        chain_in[...] = jnp.where(unit, 1.0, 0.0).astype(BF16)

    pl.semaphore_wait(barrier, rows - 1 + sectors - 1)

    def chain_copy():
        return pltpu.make_async_remote_copy(
            src_ref=pairs.at[piece], dst_ref=chain_in, send_sem=chain_send, recv_sem=chain_recv,
            device_id=(lax.rem(row + 1, rows), sector), device_id_type=MESH)

    def left_copy(slot, target):
        return pltpu.make_async_remote_copy(
            src_ref=left_bf, dst_ref=left_in.at[slot], send_sem=left_send.at[target], recv_sem=left_recv.at[slot],
            device_id=(target, sector), device_id_type=MESH)

    def info_copy(slot, step, target):
        return pltpu.make_async_remote_copy(
            src_ref=info.at[slot], dst_ref=info.at[slot], send_sem=info_send.at[step], recv_sem=info_recv.at[slot],
            device_id=(row, target), device_id_type=MESH)

    def pair_copy(slot, step, target):
        return pltpu.make_async_remote_copy(
            src_ref=pairs.at[slot], dst_ref=pairs.at[slot], send_sem=pair_send.at[step], recv_sem=pair_recv.at[slot],
            device_id=(row, target), device_id_type=MESH)

    def y_copy(slot, sem, target):
        return pltpu.make_async_remote_copy(
            src_ref=ys.at[slot], dst_ref=ys.at[slot], send_sem=sem, recv_sem=y_recv.at[slot],
            device_id=(row, target), device_id_type=MESH)

    for target in range(rows - 1, 0, -1):
        @pl.when(row < target)
        def _():
            left_copy(row, target).start()
    for step in range(1, sectors):
        info_copy(sector, step, lax.rem(sector + step, sectors)).start()

    @pl.when(row > 0)
    def _():
        chain_copy().wait_recv()
    before = chain_in[...]
    product = 0.9 * before.astype(F32) + jnp.dot(before, right_bf[...], preferred_element_type=F32)
    pairs[piece] = product.astype(BF16)

    @pl.when(row < rows - 1)
    def _():
        chain_copy().start()
    for step in range(1, slices):
        pair_copy(piece, step, group_base + partner(piece, step, slices)[0]).start()

    y_f32[...] = jnp.where(kept, boundary_in[0], 0.0)

    def apply_left(factor):
        value = y_f32[...]
        moved = jnp.dot(factor, value.astype(BF16), preferred_element_type=F32)
        return jnp.where(kept, 0.9 * value + moved, 0.0)

    for source in range(rows - 1):
        @pl.when(source < row)
        def _():
            left_copy(source, source + 1).wait_recv()
            y_f32[...] = apply_left(left_in[source])
    ys[sector] = apply_left(left_bf[...]).astype(BF16)

    for step in range(groups - 1, 0, -1):
        y_copy(sector, y_send.at[step], partner(group, step, groups)[0] * 2 + core).start()
    y_copy(sector, y_send.at[0], twin).start()

    for step in range(1, sectors):
        source = lax.rem(sector + step, sectors)
        info_copy(source, step, source).wait_recv()
    me = sector.astype(F32)
    for source in range(sectors):
        picked = jnp.zeros((width, width), BF16)
        for j in range(slots):
            mark = info[source, pl.ds(j, 1), :]
            mark = jnp.concatenate([mark] * (width // 128), axis=1)
            same = jnp.where(mark == me, 1.0, 0.0).astype(BF16)
            picked = picked + weight[0, j] * same
        chosen[source] = picked

    for step in range(groups - 1, 0, -1):
        slot = partner(group, step, groups)[1] * 2 + core
        y_copy(slot, y_send.at[step], slot).wait_recv()
        y_copy(slot, twin_send.at[step], twin).start()

    for step in range(1, slices):
        slot = partner(piece, step, slices)[1]
        pair_copy(slot, step, group_base + slot).wait_recv()
    all_pairs = pairs[...].reshape(width, width)

    def term(slot, first=False):
        moved = jnp.dot(ys[slot], all_pairs, preferred_element_type=F32)
        if first:
            bound_out[0, 0] = moved
        return jnp.dot(moved.astype(BF16), chosen[slot], preferred_element_type=F32).astype(BF16).astype(F32)

    total = term(sector, True)
    for step in range(groups - 1, 0, -1):
        total = total + term(partner(group, step, groups)[1] * 2 + core)
    y_copy(twin, y_send.at[0], twin).wait_recv()
    total = total + term(twin)
    for step in range(groups - 1, 0, -1):
        slot = partner(group, step, groups)[1] * 2 + 1 - core
        y_copy(slot, twin_send.at[step], twin).wait_recv()
        total = total + term(slot)
    env_out[0, 0] = total

    for target in range(1, rows):
        @pl.when(row < target)
        def _():
            left_copy(row, target).wait_send()

    @pl.when(row < rows - 1)
    def _():
        chain_copy().wait_send()
    for step in range(1, sectors):
        info_copy(sector, step, lax.rem(sector + step, sectors)).wait_send()
    for step in range(1, slices):
        pair_copy(piece, step, group_base + partner(piece, step, slices)[0]).wait_send()
    y_copy(sector, y_send.at[0], twin).wait_send()
    for step in range(1, groups):
        y_copy(sector, y_send.at[step], partner(group, step, groups)[0] * 2 + core).wait_send()
        y_copy(partner(group, step, groups)[1] * 2 + core, twin_send.at[step], twin).wait_send()


def solution(mesh):
    rows, sectors = mesh.shape["row"], mesh.shape["sector"]

    def on_device(boundary_in, left, right, weight, ranks, routes, owner):
        block, width = boundary_in.shape[1:]
        slots = weight.shape[1]
        slices = min(sectors, width // 16)
        out = jax.ShapeDtypeStruct((1, 1, block, width), F32)
        vmem, smem = pl.BlockSpec(memory_space=pltpu.VMEM), pl.BlockSpec(memory_space=pltpu.SMEM)
        dma = pltpu.SemaphoreType.DMA
        return pl.pallas_call(
            functools.partial(kernel, rows, sectors, slices),
            out_shape=(out, out),
            in_specs=[smem] * 3 + [vmem] * 4,
            out_specs=(vmem, vmem),
            scratch_shapes=[
                pltpu.VMEM((block, block), BF16),
                pltpu.VMEM((rows - 1, block, block), BF16),
                pltpu.VMEM((width, width), BF16),
                pltpu.VMEM((block, width), F32),
                pltpu.VMEM((width // slices, width), BF16),
                pltpu.VMEM((slices, width // slices, width), BF16),
                pltpu.VMEM((sectors, block, width), BF16),
                pltpu.VMEM((sectors, max(8, slots), 128), F32),
                pltpu.VMEM((sectors, width, width), BF16),
                dma((rows,)), dma((rows,)), dma, dma, dma((slices,)), dma((slices,)),
                dma((sectors // 2,)), dma((sectors,)), dma((sectors // 2,)), dma((sectors,)), dma((sectors,)),
            ],
            compiler_params=pltpu.CompilerParams(
                collective_id=0, has_side_effects=True, vmem_limit_bytes=32 * 2**20),
        )(ranks, routes, owner, boundary_in, left, right, weight)

    return jax.shard_map(
        on_device,
        mesh=mesh,
        in_specs=(
            P("sector", None, None),
            P("row", "sector", None, None),
            P("row", None, None),
            P("row", None, None, None),
            P("sector"),
            P("sector", None),
            P(),
        ),
        out_specs=(P("row", "sector", None, None), P("row", "sector", None, None)),
        check_vma=False,
    )
```

```python
import functools

import jax
import jax.numpy as jnp
from jax import lax
from jax.experimental import pallas as pl
from jax.experimental.pallas import tpu as pltpu
from jax.sharding import PartitionSpec as P

MESH = pl.DeviceIdType.MESH
BF16 = jnp.bfloat16
F32 = jnp.float32


def partner(index, step, count):
    if count & (count - 1):
        return lax.rem(index + step, count), lax.rem(index - step + count, count)
    result, bit = 0, 1
    while bit < count:
        own = lax.rem(index // bit, 2)
        result = result + ((1 - own) if step & bit else own) * bit
        bit *= 2
    return result, result


def kernel(
    rows, sectors, slices,
    ranks_hbm, routes_hbm, owner_hbm, boundary_hbm, left_hbm, right_hbm, weight_hbm,
    bound_out, env_out,
    ranks, routes, owner, boundary, left, right, weight, in_sem,
    left_bf, left_in, right_bf, product, chain_in, pairs, starts, prefixes, moved, info, chosen,
    left_send, left_recv, chain_send, chain_recv, pair_send, pair_recv,
    start_send, start_recv, start_twin, prefix_send, prefix_recv, prefix_twin, info_send, info_recv,
):
    row, sector = lax.axis_index("row"), lax.axis_index("sector")
    slots = weight.shape[1]
    block, width = boundary.shape[1], boundary.shape[2]
    piece_rows = width // slices
    piece = lax.rem(sector, slices)
    group_base = sector - piece
    groups = sectors // 2
    group, core = sector // 2, lax.rem(sector, 2)
    twin = group * 2 + 1 - core

    barrier = pltpu.get_barrier_semaphore()
    for step in range(1, rows):
        pl.semaphore_signal(barrier, inc=1, device_id=(lax.rem(row + step, rows), sector), device_id_type=MESH)
    for step in range(1, sectors):
        pl.semaphore_signal(barrier, inc=1, device_id=(row, lax.rem(sector + step, sectors)), device_id_type=MESH)

    loads = [
        pltpu.make_async_copy(source, target, in_sem.at[at])
        for at, (source, target) in enumerate((
            (right_hbm, right), (left_hbm, left), (boundary_hbm, boundary), (ranks_hbm, ranks),
            (routes_hbm, routes), (owner_hbm, owner), (weight_hbm, weight)))
    ]
    for load in loads:
        load.start()
    loads[0].wait()
    right_bf[...] = right[0].astype(BF16)
    loads[1].wait()
    left_bf[...] = left[0, 0].astype(BF16)
    loads[2].wait()
    starts[sector] = boundary[0].astype(BF16)
    for load in loads[3:6]:
        load.wait()
    for j in range(slots):
        info[sector, pl.ds(j, 1), :] = jnp.full((1, 128), owner[routes[0, j]], jnp.int32).astype(F32)

    @pl.when(row == 0)
    def _():
        at = lax.broadcasted_iota(jnp.int32, (piece_rows, width), 0) + piece * piece_rows
        unit = at == lax.broadcasted_iota(jnp.int32, (piece_rows, width), 1)
        chain_in[...] = jnp.where(unit, 1.0, 0.0).astype(BF16)

    pl.semaphore_wait(barrier, rows - 1 + sectors - 1)

    def chain_copy():
        return pltpu.make_async_remote_copy(
            src_ref=pairs.at[piece], dst_ref=chain_in, send_sem=chain_send, recv_sem=chain_recv,
            device_id=(lax.rem(row + 1, rows), sector), device_id_type=MESH)

    def left_copy(slot, target):
        return pltpu.make_async_remote_copy(
            src_ref=left_bf, dst_ref=left_in.at[slot], send_sem=left_send.at[target], recv_sem=left_recv.at[slot],
            device_id=(target, sector), device_id_type=MESH)

    def in_plane(buffer, slot, send_sem, recv_sem, target):
        return pltpu.make_async_remote_copy(
            src_ref=buffer.at[slot], dst_ref=buffer.at[slot], send_sem=send_sem, recv_sem=recv_sem.at[slot],
            device_id=(row, target), device_id_type=MESH)

    def info_copy(slot, step, target):
        return in_plane(info, slot, info_send.at[step], info_recv, target)

    def pair_copy(slot, step, target):
        return in_plane(pairs, slot, pair_send.at[step], pair_recv, target)

    def start_copy(slot, sem, target):
        return in_plane(starts, slot, sem, start_recv, target)

    def prefix_copy(slot, sem, target):
        return in_plane(prefixes, slot, sem, prefix_recv, target)

    def chain_step():
        @pl.when(row > 0)
        def _():
            chain_copy().wait_recv()
        before = chain_in[...]
        after = 0.9 * before.astype(F32) + jnp.dot(before, right_bf[...], preferred_element_type=F32)
        pairs[piece] = after.astype(BF16)

        @pl.when(row < rows - 1)
        def _():
            chain_copy().start()
        for step in range(1, slices):
            pair_copy(piece, step, group_base + partner(piece, step, slices)[0]).start()

    pl.when(row == 0)(chain_step)

    for target in range(rows - 1, 0, -1):
        @pl.when(row < target)
        def _():
            left_copy(row, target).start()
    for step in range(groups - 1, 0, -1):
        start_copy(sector, start_send.at[step], partner(group, step, groups)[0] * 2 + core).start()
    start_copy(sector, start_send.at[0], twin).start()
    for step in range(1, sectors):
        info_copy(sector, step, lax.rem(sector + step, sectors)).start()

    pl.when((row > 0) & (row < rows - 1))(chain_step)

    across = lax.broadcasted_iota(jnp.int32, (block, block), 1)
    down = lax.broadcasted_iota(jnp.int32, (block, block), 0)
    kept = across < ranks[0]
    own = jnp.where(across == down, 0.9, 0.0) + left[0, 0]
    product[...] = jnp.where(kept & (down < ranks[0]), own, 0.0)
    for source in range(rows - 2, -1, -1):
        @pl.when(source < row)
        def _():
            left_copy(source, source + 1).wait_recv()
            value = product[...]
            change = jnp.dot(value.astype(BF16), left_in[source], preferred_element_type=F32)
            product[...] = jnp.where(kept, 0.9 * value + change, 0.0)
    prefixes[sector] = product[...].astype(BF16)
    for step in range(groups - 1, 0, -1):
        prefix_copy(sector, prefix_send.at[step], partner(group, step, groups)[0] * 2 + core).start()
    prefix_copy(sector, prefix_send.at[0], twin).start()

    pl.when((row > 0) & (row == rows - 1))(chain_step)

    for step in range(groups - 1, 0, -1):
        slot = partner(group, step, groups)[1] * 2 + core
        start_copy(slot, start_send.at[step], slot).wait_recv()
        start_copy(slot, start_twin.at[step], twin).start()

    loads[6].wait()
    for step in range(1, sectors):
        source = lax.rem(sector + step, sectors)
        info_copy(source, step, source).wait_recv()
    me = sector.astype(F32)
    for source in range(sectors):
        picked = jnp.zeros((width, width), BF16)
        for j in range(slots):
            mark = info[source, pl.ds(j, 1), :]
            mark = jnp.concatenate([mark] * (width // 128), axis=1)
            same = jnp.where(mark == me, 1.0, 0.0).astype(BF16)
            picked = picked + weight[0, j] * same
        chosen[source] = picked

    for step in range(groups - 1, 0, -1):
        slot = partner(group, step, groups)[1] * 2 + core
        prefix_copy(slot, prefix_send.at[step], slot).wait_recv()
        prefix_copy(slot, prefix_twin.at[step], twin).start()

    start_copy(twin, start_send.at[0], twin).wait_recv()
    for step in range(groups - 1, 0, -1):
        start_copy(partner(group, step, groups)[1] * 2 + 1 - core, start_twin.at[step], twin).wait_recv()
    for step in range(1, slices):
        slot = partner(piece, step, slices)[1]
        pair_copy(slot, step, group_base + slot).wait_recv()
    all_pairs = pairs[...].reshape(width, width)
    for source in range(sectors):
        moved[source] = jnp.dot(starts[source], all_pairs, preferred_element_type=F32).astype(BF16)

    def term(slot, first=False):
        value = jnp.dot(prefixes[slot], moved[slot], preferred_element_type=F32)
        if first:
            bound_out[0, 0] = value
        return jnp.dot(value.astype(BF16), chosen[slot], preferred_element_type=F32).astype(BF16).astype(F32)

    total = term(sector, True)
    for step in range(groups - 1, 0, -1):
        total = total + term(partner(group, step, groups)[1] * 2 + core)
    prefix_copy(twin, prefix_send.at[0], twin).wait_recv()
    total = total + term(twin)
    for step in range(groups - 1, 0, -1):
        slot = partner(group, step, groups)[1] * 2 + 1 - core
        prefix_copy(slot, prefix_twin.at[step], twin).wait_recv()
        total = total + term(slot)
    env_out[0, 0] = total

    for target in range(1, rows):
        @pl.when(row < target)
        def _():
            left_copy(row, target).wait_send()

    @pl.when(row < rows - 1)
    def _():
        chain_copy().wait_send()
    for step in range(1, sectors):
        info_copy(sector, step, lax.rem(sector + step, sectors)).wait_send()
    for step in range(1, slices):
        pair_copy(piece, step, group_base + partner(piece, step, slices)[0]).wait_send()
    for copy, first, second in ((start_copy, start_send, start_twin), (prefix_copy, prefix_send, prefix_twin)):
        copy(sector, first.at[0], twin).wait_send()
        for step in range(1, groups):
            to, source = partner(group, step, groups)
            copy(sector, first.at[step], to * 2 + core).wait_send()
            copy(source * 2 + core, second.at[step], twin).wait_send()


def solution(mesh):
    rows, sectors = mesh.shape["row"], mesh.shape["sector"]

    def on_device(boundary_in, left, right, weight, ranks, routes, owner):
        block, width = boundary_in.shape[1:]
        slots = weight.shape[1]
        slices = min(sectors, width // 16)
        out = jax.ShapeDtypeStruct((1, 1, block, width), F32)
        vmem = pl.BlockSpec(memory_space=pltpu.VMEM)
        dma = pltpu.SemaphoreType.DMA
        operands = (ranks, routes, owner, boundary_in, left, right, weight)
        return pl.pallas_call(
            functools.partial(kernel, rows, sectors, slices),
            out_shape=(out, out),
            in_specs=[pl.BlockSpec(memory_space=pltpu.HBM)] * len(operands),
            out_specs=(vmem, vmem),
            scratch_shapes=[
                *(pltpu.SMEM(operand.shape, operand.dtype) for operand in operands[:3]),
                *(pltpu.VMEM(operand.shape, operand.dtype) for operand in operands[3:]),
                dma((len(operands),)),
                pltpu.VMEM((block, block), BF16),
                pltpu.VMEM((rows - 1, block, block), BF16),
                pltpu.VMEM((width, width), BF16),
                pltpu.VMEM((block, block), F32),
                pltpu.VMEM((width // slices, width), BF16),
                pltpu.VMEM((slices, width // slices, width), BF16),
                pltpu.VMEM((sectors, block, width), BF16),
                pltpu.VMEM((sectors, block, block), BF16),
                pltpu.VMEM((sectors, block, width), BF16),
                pltpu.VMEM((sectors, max(8, slots), 128), F32),
                pltpu.VMEM((sectors, width, width), BF16),
                dma((rows,)), dma((rows,)), dma, dma, dma((slices,)), dma((slices,)),
                dma((sectors // 2,)), dma((sectors,)), dma((sectors // 2,)),
                dma((sectors // 2,)), dma((sectors,)), dma((sectors // 2,)),
                dma((sectors,)), dma((sectors,)),
            ],
            compiler_params=pltpu.CompilerParams(
                collective_id=0, has_side_effects=True, vmem_limit_bytes=60 * 2**20),
        )(*operands)

    return jax.shard_map(
        on_device,
        mesh=mesh,
        in_specs=(
            P("sector", None, None),
            P("row", "sector", None, None),
            P("row", None, None),
            P("row", None, None, None),
            P("sector"),
            P("sector", None),
            P(),
        ),
        out_specs=(P("row", "sector", None, None), P("row", "sector", None, None)),
        check_vma=False,
    )
```

```python
import functools

import jax
import jax.numpy as jnp
from jax import lax
from jax.experimental import pallas as pl
from jax.experimental.pallas import tpu as pltpu
from jax.sharding import PartitionSpec as P

MESH = pl.DeviceIdType.MESH
BF16 = jnp.bfloat16
F32 = jnp.float32


def partner(index, step, count):
    if count & (count - 1):
        return lax.rem(index + step, count), lax.rem(index - step + count, count)
    result, bit = 0, 1
    while bit < count:
        own = lax.rem(index // bit, 2)
        result = result + ((1 - own) if step & bit else own) * bit
        bit *= 2
    return result, result


def kernel(
    rows, sectors, slices,
    ranks_hbm, routes_hbm, owner_hbm, boundary_hbm, left_hbm, right_hbm, weight_hbm,
    bound_out, env_out,
    ranks, routes, owner, boundary, left, right, weight, in_sem,
    left_bf, left_in, right_bf, product, chain_in, pairs, starts, prefixes, moved, terms, info, chosen,
    left_send, left_recv, chain_send, chain_recv, pair_send, pair_recv,
    start_send, start_recv, start_twin, prefix_send, prefix_recv, prefix_twin, info_send, info_recv,
):
    row, sector = lax.axis_index("row"), lax.axis_index("sector")
    slots = weight.shape[1]
    block, width = boundary.shape[1], boundary.shape[2]
    piece_rows = width // slices
    piece = lax.rem(sector, slices)
    group_base = sector - piece
    groups = sectors // 2
    group, core = sector // 2, lax.rem(sector, 2)
    twin = group * 2 + 1 - core

    barrier = pltpu.get_barrier_semaphore()
    for step in range(1, rows):
        pl.semaphore_signal(barrier, inc=1, device_id=(lax.rem(row + step, rows), sector), device_id_type=MESH)
    for step in range(1, sectors):
        pl.semaphore_signal(barrier, inc=1, device_id=(row, lax.rem(sector + step, sectors)), device_id_type=MESH)

    loads = [
        pltpu.make_async_copy(source, target, in_sem.at[at])
        for at, (source, target) in enumerate((
            (right_hbm, right), (left_hbm, left), (boundary_hbm, boundary), (ranks_hbm, ranks),
            (routes_hbm, routes), (owner_hbm, owner), (weight_hbm, weight)))
    ]
    for load in loads:
        load.start()
    loads[0].wait()
    right_bf[...] = right[0].astype(BF16)
    loads[1].wait()
    left_bf[...] = left[0, 0].astype(BF16)
    loads[2].wait()
    starts[sector] = boundary[0].astype(BF16)
    for load in loads[3:6]:
        load.wait()
    for j in range(slots):
        info[sector, pl.ds(j, 1), :] = jnp.full((1, 128), owner[routes[0, j]], jnp.int32).astype(F32)

    @pl.when(row == 0)
    def _():
        at = lax.broadcasted_iota(jnp.int32, (piece_rows, width), 0) + piece * piece_rows
        unit = at == lax.broadcasted_iota(jnp.int32, (piece_rows, width), 1)
        chain_in[...] = jnp.where(unit, 1.0, 0.0).astype(BF16)

    pl.semaphore_wait(barrier, rows - 1 + sectors - 1)

    def chain_copy():
        return pltpu.make_async_remote_copy(
            src_ref=pairs.at[piece], dst_ref=chain_in, send_sem=chain_send, recv_sem=chain_recv,
            device_id=(lax.rem(row + 1, rows), sector), device_id_type=MESH)

    def left_copy(slot, target):
        return pltpu.make_async_remote_copy(
            src_ref=left_bf, dst_ref=left_in.at[slot], send_sem=left_send.at[target], recv_sem=left_recv.at[slot],
            device_id=(target, sector), device_id_type=MESH)

    def in_plane(buffer, slot, send_sem, recv_sem, target):
        return pltpu.make_async_remote_copy(
            src_ref=buffer.at[slot], dst_ref=buffer.at[slot], send_sem=send_sem, recv_sem=recv_sem.at[slot],
            device_id=(row, target), device_id_type=MESH)

    def info_copy(slot, step, target):
        return in_plane(info, slot, info_send.at[step], info_recv, target)

    def pair_copy(slot, step, target):
        return in_plane(pairs, slot, pair_send.at[step], pair_recv, target)

    def start_copy(slot, sem, target):
        return in_plane(starts, slot, sem, start_recv, target)

    def prefix_copy(slot, sem, target):
        return in_plane(prefixes, slot, sem, prefix_recv, target)

    def chain_step():
        @pl.when(row > 0)
        def _():
            chain_copy().wait_recv()
        before = chain_in[...]
        after = 0.9 * before.astype(F32) + jnp.dot(before, right_bf[...], preferred_element_type=F32)
        pairs[piece] = after.astype(BF16)

        @pl.when(row < rows - 1)
        def _():
            chain_copy().start()
        for step in range(1, slices):
            pair_copy(piece, step, group_base + partner(piece, step, slices)[0]).start()

    pl.when(row == 0)(chain_step)

    for target in range(rows - 1, 0, -1):
        @pl.when(row < target)
        def _():
            left_copy(row, target).start()
    for step in range(groups - 1, 0, -1):
        start_copy(sector, start_send.at[step], partner(group, step, groups)[0] * 2 + core).start()
    start_copy(sector, start_send.at[0], twin).start()
    for step in range(1, sectors):
        info_copy(sector, step, lax.rem(sector + step, sectors)).start()

    pl.when((row > 0) & (row < rows - 1))(chain_step)

    loads[6].wait()
    for step in range(1, sectors):
        source = lax.rem(sector + step, sectors)
        info_copy(source, step, source).wait_recv()
    me = sector.astype(F32)
    for source in range(sectors):
        picked = jnp.zeros((width, width), BF16)
        for j in range(slots):
            mark = info[source, pl.ds(j, 1), :]
            mark = jnp.concatenate([mark] * (width // 128), axis=1)
            same = jnp.where(mark == me, 1.0, 0.0).astype(BF16)
            picked = picked + weight[0, j] * same
        chosen[source] = picked

    across = lax.broadcasted_iota(jnp.int32, (block, block), 1)
    down = lax.broadcasted_iota(jnp.int32, (block, block), 0)
    kept = across < ranks[0]
    own = jnp.where(across == down, 0.9, 0.0) + left[0, 0]
    product[...] = jnp.where(kept & (down < ranks[0]), own, 0.0)
    for source in range(rows - 2, -1, -1):
        @pl.when(source < row)
        def _():
            left_copy(source, source + 1).wait_recv()
            value = product[...]
            change = jnp.dot(value.astype(BF16), left_in[source], preferred_element_type=F32)
            product[...] = jnp.where(kept, 0.9 * value + change, 0.0)
    prefixes[sector] = product[...].astype(BF16)
    for step in range(groups - 1, 0, -1):
        prefix_copy(sector, prefix_send.at[step], partner(group, step, groups)[0] * 2 + core).start()
    prefix_copy(sector, prefix_send.at[0], twin).start()

    pl.when((row > 0) & (row == rows - 1))(chain_step)

    for step in range(groups - 1, 0, -1):
        slot = partner(group, step, groups)[1] * 2 + core
        start_copy(slot, start_send.at[step], slot).wait_recv()
        start_copy(slot, start_twin.at[step], twin).start()

    for step in range(groups - 1, 0, -1):
        slot = partner(group, step, groups)[1] * 2 + core
        prefix_copy(slot, prefix_send.at[step], slot).wait_recv()
        prefix_copy(slot, prefix_twin.at[step], twin).start()

    start_copy(twin, start_send.at[0], twin).wait_recv()
    for step in range(groups - 1, 0, -1):
        start_copy(partner(group, step, groups)[1] * 2 + 1 - core, start_twin.at[step], twin).wait_recv()
    for step in range(1, slices):
        slot = partner(piece, step, slices)[1]
        pair_copy(slot, step, group_base + slot).wait_recv()
    all_pairs = pairs[...].reshape(width, width)
    for source in range(sectors):
        value = jnp.dot(starts[source], all_pairs, preferred_element_type=F32).astype(BF16)
        moved[source] = value
        terms[source] = jnp.dot(value, chosen[source], preferred_element_type=F32).astype(BF16)
    bound_out[0, 0] = jnp.dot(prefixes[sector], moved[sector], preferred_element_type=F32)

    prefix_copy(twin, prefix_send.at[0], twin).wait_recv()
    for step in range(groups - 1, 0, -1):
        prefix_copy(partner(group, step, groups)[1] * 2 + 1 - core, prefix_twin.at[step], twin).wait_recv()
    total = jnp.zeros((block, width), F32)
    for first in range(0, sectors, 2):
        both = jnp.concatenate([prefixes[first], prefixes[first + 1]], axis=1)
        total = total + jnp.dot(
            both, terms[pl.ds(first, 2)].reshape(2 * block, width), preferred_element_type=F32)
    env_out[0, 0] = total

    for target in range(1, rows):
        @pl.when(row < target)
        def _():
            left_copy(row, target).wait_send()

    @pl.when(row < rows - 1)
    def _():
        chain_copy().wait_send()
    for step in range(1, sectors):
        info_copy(sector, step, lax.rem(sector + step, sectors)).wait_send()
    for step in range(1, slices):
        pair_copy(piece, step, group_base + partner(piece, step, slices)[0]).wait_send()
    for copy, first, second in ((start_copy, start_send, start_twin), (prefix_copy, prefix_send, prefix_twin)):
        copy(sector, first.at[0], twin).wait_send()
        for step in range(1, groups):
            to, source = partner(group, step, groups)
            copy(sector, first.at[step], to * 2 + core).wait_send()
            copy(source * 2 + core, second.at[step], twin).wait_send()


def solution(mesh):
    rows, sectors = mesh.shape["row"], mesh.shape["sector"]

    def on_device(boundary_in, left, right, weight, ranks, routes, owner):
        block, width = boundary_in.shape[1:]
        slots = weight.shape[1]
        slices = min(sectors, width // 16)
        out = pltpu.VMEM((1, 1, block, width), F32)
        vmem = pl.BlockSpec(memory_space=pltpu.VMEM)
        dma = pltpu.SemaphoreType.DMA
        operands = (ranks, routes, owner, boundary_in, left, right, weight)
        return pl.pallas_call(
            functools.partial(kernel, rows, sectors, slices),
            out_shape=(out, out),
            in_specs=[pl.BlockSpec(memory_space=pltpu.HBM)] * len(operands),
            out_specs=(vmem, vmem),
            scratch_shapes=[
                *(pltpu.SMEM(operand.shape, operand.dtype) for operand in operands[:3]),
                *(pltpu.VMEM(operand.shape, operand.dtype) for operand in operands[3:]),
                dma((len(operands),)),
                pltpu.VMEM((block, block), BF16),
                pltpu.VMEM((rows - 1, block, block), BF16),
                pltpu.VMEM((width, width), BF16),
                pltpu.VMEM((block, block), F32),
                pltpu.VMEM((width // slices, width), BF16),
                pltpu.VMEM((slices, width // slices, width), BF16),
                pltpu.VMEM((sectors, block, width), BF16),
                pltpu.VMEM((sectors, block, block), BF16),
                pltpu.VMEM((sectors, block, width), BF16),
                pltpu.VMEM((sectors, block, width), BF16),
                pltpu.VMEM((sectors, max(8, slots), 128), F32),
                pltpu.VMEM((sectors, width, width), BF16),
                dma((rows,)), dma((rows,)), dma, dma, dma((slices,)), dma((slices,)),
                dma((sectors // 2,)), dma((sectors,)), dma((sectors // 2,)),
                dma((sectors // 2,)), dma((sectors,)), dma((sectors // 2,)),
                dma((sectors,)), dma((sectors,)),
            ],
            compiler_params=pltpu.CompilerParams(
                collective_id=0, has_side_effects=True, vmem_limit_bytes=60 * 2**20),
        )(*operands)

    return jax.shard_map(
        on_device,
        mesh=mesh,
        in_specs=(
            P("sector", None, None),
            P("row", "sector", None, None),
            P("row", None, None),
            P("row", None, None, None),
            P("sector"),
            P("sector", None),
            P(),
        ),
        out_specs=(P("row", "sector", None, None), P("row", "sector", None, None)),
        check_vma=False,
    )
```

```python
import functools

import jax
import jax.numpy as jnp
from jax import lax
from jax.experimental import pallas as pl
from jax.experimental.pallas import tpu as pltpu
from jax.sharding import PartitionSpec as P

MESH = pl.DeviceIdType.MESH
BF16 = jnp.bfloat16
F32 = jnp.float32


def partner(index, step, count):
    if count & (count - 1):
        return lax.rem(index + step, count), lax.rem(index - step + count, count)
    result, bit = 0, 1
    while bit < count:
        own = lax.rem(index // bit, 2)
        result = result + ((1 - own) if step & bit else own) * bit
        bit *= 2
    return result, result


def kernel(
    rows, sectors, slices,
    ranks_hbm, routes_hbm, owner_hbm, boundary_hbm, left_hbm, right_hbm, weight_hbm,
    bound_out, env_out,
    ranks, routes, owner, boundary, left, right, weight, in_sem,
    left_bf, left_in, right_bf, product, chain_in, pairs, starts, prefixes, moved, terms, info, chosen,
    left_send, left_recv, chain_send, chain_recv, pair_send, pair_recv,
    start_send, start_recv, start_twin, prefix_send, prefix_recv, prefix_twin, info_send, info_recv,
):
    row, sector = lax.axis_index("row"), lax.axis_index("sector")
    slots = weight.shape[1]
    block, width = boundary.shape[1], boundary.shape[2]
    piece_rows = width // slices
    piece = lax.rem(sector, slices)
    group_base = sector - piece
    groups = sectors // 2
    group, core = sector // 2, lax.rem(sector, 2)
    twin = group * 2 + 1 - core

    barrier = pltpu.get_barrier_semaphore()
    for step in range(1, rows):
        pl.semaphore_signal(barrier, inc=1, device_id=(lax.rem(row + step, rows), sector), device_id_type=MESH)
    for step in range(1, sectors):
        pl.semaphore_signal(barrier, inc=1, device_id=(row, lax.rem(sector + step, sectors)), device_id_type=MESH)

    loads = [
        pltpu.make_async_copy(source, target, in_sem.at[at])
        for at, (source, target) in enumerate((
            (right_hbm, right), (left_hbm, left), (boundary_hbm, boundary), (ranks_hbm, ranks),
            (routes_hbm, routes), (owner_hbm, owner), (weight_hbm, weight)))
    ]
    for load in loads:
        load.start()
    loads[0].wait()
    right_bf[...] = right[0].astype(BF16)
    loads[1].wait()
    left_bf[...] = left[0, 0].astype(BF16)
    loads[2].wait()
    starts[sector] = boundary[0].astype(BF16)
    for load in loads[3:6]:
        load.wait()
    for j in range(slots):
        info[sector, pl.ds(j, 1), :] = jnp.full((1, 128), owner[routes[0, j]], jnp.int32).astype(F32)

    @pl.when(row == 0)
    def _():
        masked = jnp.where(lax.broadcasted_iota(jnp.int32, (block, width), 0) < ranks[0], boundary[0], 0.0)
        change = jnp.dot(left_bf[...], masked.astype(BF16), preferred_element_type=F32)
        full = jnp.where(
            lax.broadcasted_iota(jnp.int32, (block, width), 0) < ranks[0], 0.9 * masked + change, 0.0)
        starts[sector] = full.astype(BF16)
        at = lax.broadcasted_iota(jnp.int32, (piece_rows, width), 0) + piece * piece_rows
        unit = at == lax.broadcasted_iota(jnp.int32, (piece_rows, width), 1)
        chain_in[...] = jnp.where(unit, 1.0, 0.0).astype(BF16)

    pl.semaphore_wait(barrier, rows - 1 + sectors - 1)

    def chain_copy():
        return pltpu.make_async_remote_copy(
            src_ref=pairs.at[piece], dst_ref=chain_in, send_sem=chain_send, recv_sem=chain_recv,
            device_id=(lax.rem(row + 1, rows), sector), device_id_type=MESH)

    def left_copy(slot, target):
        return pltpu.make_async_remote_copy(
            src_ref=left_bf, dst_ref=left_in.at[slot], send_sem=left_send.at[target], recv_sem=left_recv.at[slot],
            device_id=(target, sector), device_id_type=MESH)

    def in_plane(buffer, slot, send_sem, recv_sem, target):
        return pltpu.make_async_remote_copy(
            src_ref=buffer.at[slot], dst_ref=buffer.at[slot], send_sem=send_sem, recv_sem=recv_sem.at[slot],
            device_id=(row, target), device_id_type=MESH)

    def info_copy(slot, step, target):
        return in_plane(info, slot, info_send.at[step], info_recv, target)

    def pair_copy(slot, step, target):
        return in_plane(pairs, slot, pair_send.at[step], pair_recv, target)

    def start_copy(slot, sem, target):
        return in_plane(starts, slot, sem, start_recv, target)

    def prefix_copy(slot, sem, target):
        return in_plane(prefixes, slot, sem, prefix_recv, target)

    def chain_step():
        @pl.when(row > 0)
        def _():
            chain_copy().wait_recv()
        before = chain_in[...]
        after = 0.9 * before.astype(F32) + jnp.dot(before, right_bf[...], preferred_element_type=F32)
        pairs[piece] = after.astype(BF16)

        @pl.when(row < rows - 1)
        def _():
            chain_copy().start()
        for step in range(1, slices):
            pair_copy(piece, step, group_base + partner(piece, step, slices)[0]).start()

    pl.when(row == 0)(chain_step)

    for step in range(groups - 1, 0, -1):
        start_copy(sector, start_send.at[step], partner(group, step, groups)[0] * 2 + core).start()
    start_copy(sector, start_send.at[0], twin).start()
    for step in range(1, sectors):
        info_copy(sector, step, lax.rem(sector + step, sectors)).start()

    pl.when((row > 0) & (row < rows - 1))(chain_step)

    for target in range(rows - 1, 0, -1):
        @pl.when(row < target)
        def _():
            left_copy(row, target).start()
    loads[6].wait()
    for step in range(1, sectors):
        source = lax.rem(sector + step, sectors)
        info_copy(source, step, source).wait_recv()
    me = sector.astype(F32)
    for source in range(sectors):
        picked = jnp.zeros((width, width), BF16)
        for j in range(slots):
            mark = info[source, pl.ds(j, 1), :]
            mark = jnp.concatenate([mark] * (width // 128), axis=1)
            same = jnp.where(mark == me, 1.0, 0.0).astype(BF16)
            picked = picked + weight[0, j] * same
        chosen[source] = picked

    across = lax.broadcasted_iota(jnp.int32, (block, block), 1)
    down = lax.broadcasted_iota(jnp.int32, (block, block), 0)
    kept = across < ranks[0]
    own = jnp.where(across == down, 0.9, 0.0) + left[0, 0]
    product[...] = jnp.where(kept & (down < ranks[0]), own, 0.0)
    for source in range(rows - 2, -1, -1):
        @pl.when(source < row)
        def _():
            left_copy(source, source + 1).wait_recv()
            value = product[...]
            change = jnp.dot(value.astype(BF16), left_in[source], preferred_element_type=F32)
            product[...] = jnp.where(kept, 0.9 * value + change, 0.0)
    prefixes[sector] = product[...].astype(BF16)

    @pl.when(row > 0)
    def _():
        for step in range(groups - 1, 0, -1):
            prefix_copy(sector, prefix_send.at[step], partner(group, step, groups)[0] * 2 + core).start()
        prefix_copy(sector, prefix_send.at[0], twin).start()

    pl.when((row > 0) & (row == rows - 1))(chain_step)

    for step in range(groups - 1, 0, -1):
        slot = partner(group, step, groups)[1] * 2 + core
        start_copy(slot, start_send.at[step], slot).wait_recv()
        start_copy(slot, start_twin.at[step], twin).start()

    @pl.when(row > 0)
    def _():
        for step in range(groups - 1, 0, -1):
            slot = partner(group, step, groups)[1] * 2 + core
            prefix_copy(slot, prefix_send.at[step], slot).wait_recv()
            prefix_copy(slot, prefix_twin.at[step], twin).start()

    start_copy(twin, start_send.at[0], twin).wait_recv()
    for step in range(groups - 1, 0, -1):
        start_copy(partner(group, step, groups)[1] * 2 + 1 - core, start_twin.at[step], twin).wait_recv()
    for step in range(1, slices):
        slot = partner(piece, step, slices)[1]
        pair_copy(slot, step, group_base + slot).wait_recv()
    all_pairs = pairs[...].reshape(width, width)
    for source in range(sectors):
        value = jnp.dot(starts[source], all_pairs, preferred_element_type=F32).astype(BF16)
        moved[source] = value
        terms[source] = jnp.dot(value, chosen[source], preferred_element_type=F32).astype(BF16)

    @pl.when(row == 0)
    def _():
        bound_out[0, 0] = jnp.dot(starts[sector], all_pairs, preferred_element_type=F32)
        total = terms[0].astype(F32)
        for source in range(1, sectors):
            total = total + terms[source].astype(F32)
        env_out[0, 0] = total

    @pl.when(row > 0)
    def _():
        bound_out[0, 0] = jnp.dot(prefixes[sector], moved[sector], preferred_element_type=F32)
        prefix_copy(twin, prefix_send.at[0], twin).wait_recv()
        for step in range(groups - 1, 0, -1):
            prefix_copy(partner(group, step, groups)[1] * 2 + 1 - core, prefix_twin.at[step], twin).wait_recv()
        total = jnp.zeros((block, width), F32)
        for first in range(0, sectors, 2):
            both = jnp.concatenate([prefixes[first], prefixes[first + 1]], axis=1)
            total = total + jnp.dot(
                both, terms[pl.ds(first, 2)].reshape(2 * block, width), preferred_element_type=F32)
        env_out[0, 0] = total

    for target in range(1, rows):
        @pl.when(row < target)
        def _():
            left_copy(row, target).wait_send()

    @pl.when(row < rows - 1)
    def _():
        chain_copy().wait_send()
    for step in range(1, sectors):
        info_copy(sector, step, lax.rem(sector + step, sectors)).wait_send()
    for step in range(1, slices):
        pair_copy(piece, step, group_base + partner(piece, step, slices)[0]).wait_send()

    def all_left(copy, first, second):
        copy(sector, first.at[0], twin).wait_send()
        for step in range(1, groups):
            to, source = partner(group, step, groups)
            copy(sector, first.at[step], to * 2 + core).wait_send()
            copy(source * 2 + core, second.at[step], twin).wait_send()

    all_left(start_copy, start_send, start_twin)
    pl.when(row > 0)(functools.partial(all_left, prefix_copy, prefix_send, prefix_twin))


def solution(mesh):
    rows, sectors = mesh.shape["row"], mesh.shape["sector"]

    def on_device(boundary_in, left, right, weight, ranks, routes, owner):
        block, width = boundary_in.shape[1:]
        slots = weight.shape[1]
        slices = min(sectors, width // 16)
        out = pltpu.VMEM((1, 1, block, width), F32)
        vmem = pl.BlockSpec(memory_space=pltpu.VMEM)
        dma = pltpu.SemaphoreType.DMA
        operands = (ranks, routes, owner, boundary_in, left, right, weight)
        return pl.pallas_call(
            functools.partial(kernel, rows, sectors, slices),
            out_shape=(out, out),
            in_specs=[pl.BlockSpec(memory_space=pltpu.HBM)] * len(operands),
            out_specs=(vmem, vmem),
            scratch_shapes=[
                *(pltpu.SMEM(operand.shape, operand.dtype) for operand in operands[:3]),
                *(pltpu.VMEM(operand.shape, operand.dtype) for operand in operands[3:]),
                dma((len(operands),)),
                pltpu.VMEM((block, block), BF16),
                pltpu.VMEM((rows - 1, block, block), BF16),
                pltpu.VMEM((width, width), BF16),
                pltpu.VMEM((block, block), F32),
                pltpu.VMEM((width // slices, width), BF16),
                pltpu.VMEM((slices, width // slices, width), BF16),
                pltpu.VMEM((sectors, block, width), BF16),
                pltpu.VMEM((sectors, block, block), BF16),
                pltpu.VMEM((sectors, block, width), BF16),
                pltpu.VMEM((sectors, block, width), BF16),
                pltpu.VMEM((sectors, max(8, slots), 128), F32),
                pltpu.VMEM((sectors, width, width), BF16),
                dma((rows,)), dma((rows,)), dma, dma, dma((slices,)), dma((slices,)),
                dma((sectors // 2,)), dma((sectors,)), dma((sectors // 2,)),
                dma((sectors // 2,)), dma((sectors,)), dma((sectors // 2,)),
                dma((sectors,)), dma((sectors,)),
            ],
            compiler_params=pltpu.CompilerParams(
                collective_id=0, has_side_effects=True, vmem_limit_bytes=60 * 2**20),
        )(*operands)

    return jax.shard_map(
        on_device,
        mesh=mesh,
        in_specs=(
            P("sector", None, None),
            P("row", "sector", None, None),
            P("row", None, None),
            P("row", None, None, None),
            P("sector"),
            P("sector", None),
            P(),
        ),
        out_specs=(P("row", "sector", None, None), P("row", "sector", None, None)),
        check_vma=False,
    )
```

```python
import functools

import jax
import jax.numpy as jnp
from jax import lax
from jax.experimental import pallas as pl
from jax.experimental.pallas import tpu as pltpu
from jax.sharding import PartitionSpec as P

MESH = pl.DeviceIdType.MESH
BF16 = jnp.bfloat16
F32 = jnp.float32


def partner(index, step, count):
    if count & (count - 1):
        return lax.rem(index + step, count), lax.rem(index - step + count, count)
    result, bit = 0, 1
    while bit < count:
        own = lax.rem(index // bit, 2)
        result = result + ((1 - own) if step & bit else own) * bit
        bit *= 2
    return result, result


def kernel(
    rows, sectors, slices,
    ranks_hbm, routes_hbm, owner_hbm, boundary_hbm, left_hbm, right_hbm, weight_hbm,
    bound_out, env_out,
    ranks, routes, owner, boundary, left, right, weight, in_sem,
    left_bf, left_in, right_bf, product, chain_in, pairs, starts, prefixes, moved, terms, info, chosen,
    left_send, left_recv, chain_send, chain_recv, pair_send, pair_recv,
    start_send, start_recv, start_twin, prefix_send, prefix_recv, prefix_twin, info_send, info_recv,
):
    row, sector = lax.axis_index("row"), lax.axis_index("sector")
    slots = weight.shape[1]
    block, width = boundary.shape[1], boundary.shape[2]
    piece_rows = width // slices
    piece = lax.rem(sector, slices)
    group_base = sector - piece
    groups = sectors // 2
    group, core = sector // 2, lax.rem(sector, 2)
    twin = group * 2 + 1 - core

    barrier = pltpu.get_barrier_semaphore()
    for step in range(1, rows):
        pl.semaphore_signal(barrier, inc=1, device_id=(lax.rem(row + step, rows), sector), device_id_type=MESH)
    for step in range(1, sectors):
        pl.semaphore_signal(barrier, inc=1, device_id=(row, lax.rem(sector + step, sectors)), device_id_type=MESH)

    loads = [
        pltpu.make_async_copy(source, target, in_sem.at[at])
        for at, (source, target) in enumerate((
            (right_hbm, right), (left_hbm, left), (boundary_hbm, boundary), (ranks_hbm, ranks),
            (routes_hbm, routes), (owner_hbm, owner), (weight_hbm, weight)))
    ]
    for load in loads:
        load.start()
    loads[0].wait()
    right_bf[...] = right[0].astype(BF16)
    loads[1].wait()
    left_bf[...] = left[0, 0].astype(BF16)
    loads[2].wait()
    starts[sector] = boundary[0].astype(BF16)
    for load in loads[3:6]:
        load.wait()
    for j in range(slots):
        info[sector, pl.ds(j, 1), :] = jnp.full((1, 128), owner[routes[0, j]], jnp.int32).astype(F32)

    @pl.when(row == 0)
    def _():
        masked = jnp.where(lax.broadcasted_iota(jnp.int32, (block, width), 0) < ranks[0], boundary[0], 0.0)
        change = jnp.dot(left_bf[...], masked.astype(BF16), preferred_element_type=F32)
        full = jnp.where(
            lax.broadcasted_iota(jnp.int32, (block, width), 0) < ranks[0], 0.9 * masked + change, 0.0)
        starts[sector] = full.astype(BF16)
        at = lax.broadcasted_iota(jnp.int32, (piece_rows, width), 0) + piece * piece_rows
        unit = at == lax.broadcasted_iota(jnp.int32, (piece_rows, width), 1)
        chain_in[...] = jnp.where(unit, 1.0, 0.0).astype(BF16)

    pl.semaphore_wait(barrier, rows - 1 + sectors - 1)

    def chain_copy():
        return pltpu.make_async_remote_copy(
            src_ref=pairs.at[piece], dst_ref=chain_in, send_sem=chain_send, recv_sem=chain_recv,
            device_id=(lax.rem(row + 1, rows), sector), device_id_type=MESH)

    def left_copy(slot, target):
        return pltpu.make_async_remote_copy(
            src_ref=left_bf, dst_ref=left_in.at[slot], send_sem=left_send.at[target], recv_sem=left_recv.at[slot],
            device_id=(target, sector), device_id_type=MESH)

    def in_plane(buffer, slot, send_sem, recv_sem, target):
        return pltpu.make_async_remote_copy(
            src_ref=buffer.at[slot], dst_ref=buffer.at[slot], send_sem=send_sem, recv_sem=recv_sem.at[slot],
            device_id=(row, target), device_id_type=MESH)

    def info_copy(slot, step, target):
        return in_plane(info, slot, info_send.at[step], info_recv, target)

    def pair_copy(slot, step, target):
        return in_plane(pairs, slot, pair_send.at[step], pair_recv, target)

    def start_copy(slot, sem, target):
        return in_plane(starts, slot, sem, start_recv, target)

    def prefix_copy(slot, sem, target):
        return in_plane(prefixes, slot, sem, prefix_recv, target)

    def chain_step():
        @pl.when(row > 0)
        def _():
            chain_copy().wait_recv()
        before = chain_in[...]
        after = 0.9 * before.astype(F32) + jnp.dot(before, right_bf[...], preferred_element_type=F32)
        pairs[piece] = after.astype(BF16)

        @pl.when(row < rows - 1)
        def _():
            chain_copy().start()
        for step in range(1, slices):
            pair_copy(piece, step, group_base + partner(piece, step, slices)[0]).start()

    pl.when(row == 0)(chain_step)

    for target in range(rows - 1, 0, -1):
        @pl.when(row < target)
        def _():
            left_copy(row, target).start()
    for step in range(groups - 1, 0, -1):
        start_copy(sector, start_send.at[step], partner(group, step, groups)[0] * 2 + core).start()
    start_copy(sector, start_send.at[0], twin).start()
    for step in range(1, sectors):
        info_copy(sector, step, lax.rem(sector + step, sectors)).start()

    pl.when(row > 0)(chain_step)

    loads[6].wait()
    for step in range(1, sectors):
        source = lax.rem(sector + step, sectors)
        info_copy(source, step, source).wait_recv()
    me = sector.astype(F32)
    for source in range(sectors):
        picked = jnp.zeros((width, width), BF16)
        for j in range(slots):
            mark = info[source, pl.ds(j, 1), :]
            mark = jnp.concatenate([mark] * (width // 128), axis=1)
            same = jnp.where(mark == me, 1.0, 0.0).astype(BF16)
            picked = picked + weight[0, j] * same
        chosen[source] = picked

    across = lax.broadcasted_iota(jnp.int32, (block, block), 1)
    down = lax.broadcasted_iota(jnp.int32, (block, block), 0)
    kept = across < ranks[0]
    own = jnp.where(across == down, 0.9, 0.0) + left[0, 0]
    product[...] = jnp.where(kept & (down < ranks[0]), own, 0.0)
    for source in range(rows - 2, -1, -1):
        @pl.when(source < row)
        def _():
            left_copy(source, source + 1).wait_recv()
            value = product[...]
            change = jnp.dot(value.astype(BF16), left_in[source], preferred_element_type=F32)
            product[...] = jnp.where(kept, 0.9 * value + change, 0.0)
    prefixes[sector] = product[...].astype(BF16)

    @pl.when(row > 0)
    def _():
        for step in range(groups - 1, 0, -1):
            prefix_copy(sector, prefix_send.at[step], partner(group, step, groups)[0] * 2 + core).start()
        prefix_copy(sector, prefix_send.at[0], twin).start()

    for step in range(groups - 1, 0, -1):
        slot = partner(group, step, groups)[1] * 2 + core
        start_copy(slot, start_send.at[step], slot).wait_recv()
        start_copy(slot, start_twin.at[step], twin).start()

    @pl.when(row > 0)
    def _():
        for step in range(groups - 1, 0, -1):
            slot = partner(group, step, groups)[1] * 2 + core
            prefix_copy(slot, prefix_send.at[step], slot).wait_recv()
            prefix_copy(slot, prefix_twin.at[step], twin).start()

    start_copy(twin, start_send.at[0], twin).wait_recv()
    for step in range(groups - 1, 0, -1):
        start_copy(partner(group, step, groups)[1] * 2 + 1 - core, start_twin.at[step], twin).wait_recv()
    for step in range(1, slices):
        slot = partner(piece, step, slices)[1]
        pair_copy(slot, step, group_base + slot).wait_recv()
    all_pairs = pairs[...].reshape(width, width)
    for source in range(sectors):
        value = jnp.dot(starts[source], all_pairs, preferred_element_type=F32).astype(BF16)
        moved[source] = value
        terms[source] = jnp.dot(value, chosen[source], preferred_element_type=F32).astype(BF16)

    @pl.when(row == 0)
    def _():
        bound_out[0, 0] = jnp.dot(starts[sector], all_pairs, preferred_element_type=F32)
        total = terms[0].astype(F32)
        for source in range(1, sectors):
            total = total + terms[source].astype(F32)
        env_out[0, 0] = total

    @pl.when(row > 0)
    def _():
        bound_out[0, 0] = jnp.dot(prefixes[sector], moved[sector], preferred_element_type=F32)
        prefix_copy(twin, prefix_send.at[0], twin).wait_recv()
        for step in range(groups - 1, 0, -1):
            prefix_copy(partner(group, step, groups)[1] * 2 + 1 - core, prefix_twin.at[step], twin).wait_recv()
        total = jnp.zeros((block, width), F32)
        for first in range(0, sectors, 2):
            both = jnp.concatenate([prefixes[first], prefixes[first + 1]], axis=1)
            total = total + jnp.dot(
                both, terms[pl.ds(first, 2)].reshape(2 * block, width), preferred_element_type=F32)
        env_out[0, 0] = total

    for target in range(1, rows):
        @pl.when(row < target)
        def _():
            left_copy(row, target).wait_send()

    @pl.when(row < rows - 1)
    def _():
        chain_copy().wait_send()
    for step in range(1, sectors):
        info_copy(sector, step, lax.rem(sector + step, sectors)).wait_send()
    for step in range(1, slices):
        pair_copy(piece, step, group_base + partner(piece, step, slices)[0]).wait_send()

    def all_left(copy, first, second):
        copy(sector, first.at[0], twin).wait_send()
        for step in range(1, groups):
            to, source = partner(group, step, groups)
            copy(sector, first.at[step], to * 2 + core).wait_send()
            copy(source * 2 + core, second.at[step], twin).wait_send()

    all_left(start_copy, start_send, start_twin)
    pl.when(row > 0)(functools.partial(all_left, prefix_copy, prefix_send, prefix_twin))


def store(bound, env, bound_out, env_out, sem):
    copies = [
        pltpu.make_async_copy(bound, bound_out, sem.at[0]),
        pltpu.make_async_copy(env, env_out, sem.at[1]),
    ]
    for copy in copies:
        copy.start()
    for copy in copies:
        copy.wait()


def solution(mesh):
    rows, sectors = mesh.shape["row"], mesh.shape["sector"]

    def on_device(boundary_in, left, right, weight, ranks, routes, owner):
        block, width = boundary_in.shape[1:]
        slots = weight.shape[1]
        slices = min(sectors, width // 16)
        out = pltpu.VMEM((1, 1, block, width), F32)
        vmem = pl.BlockSpec(memory_space=pltpu.VMEM)
        dma = pltpu.SemaphoreType.DMA
        operands = (ranks, routes, owner, boundary_in, left, right, weight)
        results = pl.pallas_call(
            functools.partial(kernel, rows, sectors, slices),
            out_shape=(out, out),
            in_specs=[pl.BlockSpec(memory_space=pltpu.HBM)] * len(operands),
            out_specs=(vmem, vmem),
            scratch_shapes=[
                *(pltpu.SMEM(operand.shape, operand.dtype) for operand in operands[:3]),
                *(pltpu.VMEM(operand.shape, operand.dtype) for operand in operands[3:]),
                dma((len(operands),)),
                pltpu.VMEM((block, block), BF16),
                pltpu.VMEM((rows - 1, block, block), BF16),
                pltpu.VMEM((width, width), BF16),
                pltpu.VMEM((block, block), F32),
                pltpu.VMEM((width // slices, width), BF16),
                pltpu.VMEM((slices, width // slices, width), BF16),
                pltpu.VMEM((sectors, block, width), BF16),
                pltpu.VMEM((sectors, block, block), BF16),
                pltpu.VMEM((sectors, block, width), BF16),
                pltpu.VMEM((sectors, block, width), BF16),
                pltpu.VMEM((sectors, max(8, slots), 128), F32),
                pltpu.VMEM((sectors, width, width), BF16),
                dma((rows,)), dma((rows,)), dma, dma, dma((slices,)), dma((slices,)),
                dma((sectors // 2,)), dma((sectors,)), dma((sectors // 2,)),
                dma((sectors // 2,)), dma((sectors,)), dma((sectors // 2,)),
                dma((sectors,)), dma((sectors,)),
            ],
            compiler_params=pltpu.CompilerParams(
                collective_id=0, has_side_effects=True, vmem_limit_bytes=60 * 2**20),
        )(*operands)
        place = pl.BlockSpec(memory_space=pl.ANY)
        return pl.pallas_call(
            store,
            out_shape=(jax.ShapeDtypeStruct((1, 1, block, width), F32),) * 2,
            in_specs=[place] * 2,
            out_specs=(place,) * 2,
            scratch_shapes=[dma((2,))],
        )(*results)

    return jax.shard_map(
        on_device,
        mesh=mesh,
        in_specs=(
            P("sector", None, None),
            P("row", "sector", None, None),
            P("row", None, None),
            P("row", None, None, None),
            P("sector"),
            P("sector", None),
            P(),
        ),
        out_specs=(P("row", "sector", None, None), P("row", "sector", None, None)),
        check_vma=False,
    )
```

```python
import functools

import jax
import jax.numpy as jnp
from jax import lax
from jax.experimental import pallas as pl
from jax.experimental.pallas import tpu as pltpu
from jax.sharding import PartitionSpec as P

MESH = pl.DeviceIdType.MESH
BF16 = jnp.bfloat16
F32 = jnp.float32


def partner(index, step, count):
    if count & (count - 1):
        return lax.rem(index + step, count), lax.rem(index - step + count, count)
    result, bit = 0, 1
    while bit < count:
        own = lax.rem(index // bit, 2)
        result = result + ((1 - own) if step & bit else own) * bit
        bit *= 2
    return result, result


def kernel(
    rows, sectors, slices,
    ranks_hbm, routes_hbm, owner_hbm, boundary_hbm, left_hbm, right_hbm, weight_hbm,
    bound_out, env_out,
    ranks, routes, owner, boundary, left, right, weight, in_sem,
    left_bf, left_in, right_bf, product, chain_in, pairs, starts, prefixes, moved, terms, info, chosen,
    left_send, left_recv, chain_send, chain_recv, pair_send, pair_recv,
    start_send, start_recv, start_twin, prefix_send, prefix_recv, prefix_twin, info_send, info_recv,
):
    row, sector = lax.axis_index("row"), lax.axis_index("sector")
    slots = weight.shape[1]
    block, width = boundary.shape[1], boundary.shape[2]
    piece_rows = width // slices
    piece = lax.rem(sector, slices)
    group_base = sector - piece
    groups = sectors // 2
    group, core = sector // 2, lax.rem(sector, 2)
    twin = group * 2 + 1 - core

    barrier = pltpu.get_barrier_semaphore()
    for step in range(1, rows):
        pl.semaphore_signal(barrier, inc=1, device_id=(lax.rem(row + step, rows), sector), device_id_type=MESH)
    for step in range(1, sectors):
        pl.semaphore_signal(barrier, inc=1, device_id=(row, lax.rem(sector + step, sectors)), device_id_type=MESH)

    loads = [
        pltpu.make_async_copy(source, target, in_sem.at[at])
        for at, (source, target) in enumerate((
            (right_hbm, right), (left_hbm, left), (boundary_hbm, boundary), (ranks_hbm, ranks),
            (routes_hbm, routes), (owner_hbm, owner), (weight_hbm, weight)))
    ]
    for load in loads:
        load.start()
    loads[0].wait()
    right_bf[...] = right[0].astype(BF16)
    loads[1].wait()
    left_bf[...] = left[0, 0].astype(BF16)
    loads[2].wait()
    starts[sector] = boundary[0].astype(BF16)
    for load in loads[3:6]:
        load.wait()
    for j in range(slots):
        info[sector, pl.ds(j, 1), :] = jnp.full((1, 128), owner[routes[0, j]], jnp.int32).astype(F32)

    @pl.when(row == 0)
    def _():
        masked = jnp.where(lax.broadcasted_iota(jnp.int32, (block, width), 0) < ranks[0], boundary[0], 0.0)
        change = jnp.dot(left_bf[...], masked.astype(BF16), preferred_element_type=F32)
        full = jnp.where(
            lax.broadcasted_iota(jnp.int32, (block, width), 0) < ranks[0], 0.9 * masked + change, 0.0)
        starts[sector] = full.astype(BF16)
        at = lax.broadcasted_iota(jnp.int32, (piece_rows, width), 0) + piece * piece_rows
        unit = at == lax.broadcasted_iota(jnp.int32, (piece_rows, width), 1)
        chain_in[...] = jnp.where(unit, 1.0, 0.0).astype(BF16)

    pl.semaphore_wait(barrier, rows - 1 + sectors - 1)

    def chain_copy():
        return pltpu.make_async_remote_copy(
            src_ref=pairs.at[piece], dst_ref=chain_in, send_sem=chain_send, recv_sem=chain_recv,
            device_id=(lax.rem(row + 1, rows), sector), device_id_type=MESH)

    def left_copy(slot, target):
        return pltpu.make_async_remote_copy(
            src_ref=left_bf, dst_ref=left_in.at[slot], send_sem=left_send.at[target], recv_sem=left_recv.at[slot],
            device_id=(target, sector), device_id_type=MESH)

    def in_plane(buffer, slot, send_sem, recv_sem, target):
        return pltpu.make_async_remote_copy(
            src_ref=buffer.at[slot], dst_ref=buffer.at[slot], send_sem=send_sem, recv_sem=recv_sem.at[slot],
            device_id=(row, target), device_id_type=MESH)

    def info_copy(slot, step, target):
        return in_plane(info, slot, info_send.at[step], info_recv, target)

    def pair_copy(slot, step, target):
        return in_plane(pairs, slot, pair_send.at[step], pair_recv, target)

    def start_copy(slot, sem, target):
        return in_plane(starts, slot, sem, start_recv, target)

    def prefix_copy(slot, sem, target):
        return in_plane(prefixes, slot, sem, prefix_recv, target)

    def chain_step():
        @pl.when(row > 0)
        def _():
            chain_copy().wait_recv()
        before = chain_in[...]
        after = 0.9 * before.astype(F32) + jnp.dot(before, right_bf[...], preferred_element_type=F32)
        pairs[piece] = after.astype(BF16)

        @pl.when(row < rows - 1)
        def _():
            chain_copy().start()
        for step in range(1, slices):
            pair_copy(piece, step, group_base + partner(piece, step, slices)[0]).start()

    for target in range(rows - 1, 0, -1):
        @pl.when(row < target)
        def _():
            left_copy(row, target).start()
    pl.when(row == 0)(chain_step)

    for step in range(1, sectors):
        info_copy(sector, step, lax.rem(sector + step, sectors)).start()
    for step in range(groups - 1, 0, -1):
        start_copy(sector, start_send.at[step], partner(group, step, groups)[0] * 2 + core).start()
    start_copy(sector, start_send.at[0], twin).start()

    pl.when((row > 0) & (row < rows - 1))(chain_step)

    loads[6].wait()
    for step in range(1, sectors):
        source = lax.rem(sector + step, sectors)
        info_copy(source, step, source).wait_recv()
    me = sector.astype(F32)
    for source in range(sectors):
        picked = jnp.zeros((width, width), BF16)
        for j in range(slots):
            mark = info[source, pl.ds(j, 1), :]
            mark = jnp.concatenate([mark] * (width // 128), axis=1)
            same = jnp.where(mark == me, 1.0, 0.0).astype(BF16)
            picked = picked + weight[0, j] * same
        chosen[source] = picked

    across = lax.broadcasted_iota(jnp.int32, (block, block), 1)
    down = lax.broadcasted_iota(jnp.int32, (block, block), 0)
    kept = across < ranks[0]
    own = jnp.where(across == down, 0.9, 0.0) + left[0, 0]
    product[...] = jnp.where(kept & (down < ranks[0]), own, 0.0)
    for source in range(rows - 2, -1, -1):
        @pl.when(source < row)
        def _():
            left_copy(source, source + 1).wait_recv()
            value = product[...]
            change = jnp.dot(value.astype(BF16), left_in[source], preferred_element_type=F32)
            product[...] = jnp.where(kept, 0.9 * value + change, 0.0)
    prefixes[sector] = product[...].astype(BF16)

    @pl.when(row > 0)
    def _():
        for step in range(groups - 1, 0, -1):
            prefix_copy(sector, prefix_send.at[step], partner(group, step, groups)[0] * 2 + core).start()
        prefix_copy(sector, prefix_send.at[0], twin).start()

    pl.when((row > 0) & (row == rows - 1))(chain_step)

    for step in range(groups - 1, 0, -1):
        slot = partner(group, step, groups)[1] * 2 + core
        start_copy(slot, start_send.at[step], slot).wait_recv()
        start_copy(slot, start_twin.at[step], twin).start()

    @pl.when(row > 0)
    def _():
        for step in range(groups - 1, 0, -1):
            slot = partner(group, step, groups)[1] * 2 + core
            prefix_copy(slot, prefix_send.at[step], slot).wait_recv()
            prefix_copy(slot, prefix_twin.at[step], twin).start()

    start_copy(twin, start_send.at[0], twin).wait_recv()
    for step in range(groups - 1, 0, -1):
        start_copy(partner(group, step, groups)[1] * 2 + 1 - core, start_twin.at[step], twin).wait_recv()
    for step in range(1, slices):
        slot = partner(piece, step, slices)[1]
        pair_copy(slot, step, group_base + slot).wait_recv()
    all_pairs = pairs[...].reshape(width, width)
    for source in range(sectors):
        moved[source] = jnp.dot(starts[source], all_pairs, preferred_element_type=F32).astype(BF16)
    for source in range(sectors):
        terms[source] = jnp.dot(moved[source], chosen[source], preferred_element_type=F32).astype(BF16)

    @pl.when(row == 0)
    def _():
        bound_out[0, 0] = jnp.dot(starts[sector], all_pairs, preferred_element_type=F32)
        total = terms[0].astype(F32)
        for source in range(1, sectors):
            total = total + terms[source].astype(F32)
        env_out[0, 0] = total

    @pl.when(row > 0)
    def _():
        bound_out[0, 0] = jnp.dot(prefixes[sector], moved[sector], preferred_element_type=F32)
        prefix_copy(twin, prefix_send.at[0], twin).wait_recv()
        for step in range(groups - 1, 0, -1):
            prefix_copy(partner(group, step, groups)[1] * 2 + 1 - core, prefix_twin.at[step], twin).wait_recv()
        total = jnp.zeros((block, width), F32)
        for first in range(0, sectors, 2):
            both = jnp.concatenate([prefixes[first], prefixes[first + 1]], axis=1)
            total = total + jnp.dot(
                both, terms[pl.ds(first, 2)].reshape(2 * block, width), preferred_element_type=F32)
        env_out[0, 0] = total

    for target in range(1, rows):
        @pl.when(row < target)
        def _():
            left_copy(row, target).wait_send()

    @pl.when(row < rows - 1)
    def _():
        chain_copy().wait_send()
    for step in range(1, sectors):
        info_copy(sector, step, lax.rem(sector + step, sectors)).wait_send()
    for step in range(1, slices):
        pair_copy(piece, step, group_base + partner(piece, step, slices)[0]).wait_send()

    def all_left(copy, first, second):
        copy(sector, first.at[0], twin).wait_send()
        for step in range(1, groups):
            to, source = partner(group, step, groups)
            copy(sector, first.at[step], to * 2 + core).wait_send()
            copy(source * 2 + core, second.at[step], twin).wait_send()

    all_left(start_copy, start_send, start_twin)
    pl.when(row > 0)(functools.partial(all_left, prefix_copy, prefix_send, prefix_twin))


def solution(mesh):
    rows, sectors = mesh.shape["row"], mesh.shape["sector"]

    def on_device(boundary_in, left, right, weight, ranks, routes, owner):
        block, width = boundary_in.shape[1:]
        slots = weight.shape[1]
        slices = min(sectors, width // 16)
        out = pltpu.VMEM((1, 1, block, width), F32)
        vmem = pl.BlockSpec(memory_space=pltpu.VMEM)
        dma = pltpu.SemaphoreType.DMA
        operands = (ranks, routes, owner, boundary_in, left, right, weight)
        return pl.pallas_call(
            functools.partial(kernel, rows, sectors, slices),
            out_shape=(out, out),
            in_specs=[pl.BlockSpec(memory_space=pltpu.HBM)] * len(operands),
            out_specs=(vmem, vmem),
            scratch_shapes=[
                *(pltpu.SMEM(operand.shape, operand.dtype) for operand in operands[:3]),
                *(pltpu.VMEM(operand.shape, operand.dtype) for operand in operands[3:]),
                dma((len(operands),)),
                pltpu.VMEM((block, block), BF16),
                pltpu.VMEM((rows - 1, block, block), BF16),
                pltpu.VMEM((width, width), BF16),
                pltpu.VMEM((block, block), F32),
                pltpu.VMEM((width // slices, width), BF16),
                pltpu.VMEM((slices, width // slices, width), BF16),
                pltpu.VMEM((sectors, block, width), BF16),
                pltpu.VMEM((sectors, block, block), BF16),
                pltpu.VMEM((sectors, block, width), BF16),
                pltpu.VMEM((sectors, block, width), BF16),
                pltpu.VMEM((sectors, max(8, slots), 128), F32),
                pltpu.VMEM((sectors, width, width), BF16),
                dma((rows,)), dma((rows,)), dma, dma, dma((slices,)), dma((slices,)),
                dma((sectors // 2,)), dma((sectors,)), dma((sectors // 2,)),
                dma((sectors // 2,)), dma((sectors,)), dma((sectors // 2,)),
                dma((sectors,)), dma((sectors,)),
            ],
            compiler_params=pltpu.CompilerParams(
                collective_id=0, has_side_effects=True, vmem_limit_bytes=60 * 2**20),
        )(*operands)

    return jax.shard_map(
        on_device,
        mesh=mesh,
        in_specs=(
            P("sector", None, None),
            P("row", "sector", None, None),
            P("row", None, None),
            P("row", None, None, None),
            P("sector"),
            P("sector", None),
            P(),
        ),
        out_specs=(P("row", "sector", None, None), P("row", "sector", None, None)),
        check_vma=False,
    )
```

```python
import functools

import jax
import jax.numpy as jnp
from jax import lax
from jax.experimental import pallas as pl
from jax.experimental.pallas import tpu as pltpu
from jax.sharding import PartitionSpec as P

MESH = pl.DeviceIdType.MESH
BF16 = jnp.bfloat16
F32 = jnp.float32


def partner(index, step, count):
    if count & (count - 1):
        return lax.rem(index + step, count), lax.rem(index - step + count, count)
    result, bit = 0, 1
    while bit < count:
        own = lax.rem(index // bit, 2)
        result = result + ((1 - own) if step & bit else own) * bit
        bit *= 2
    return result, result


def kernel(
    rows, sectors, slices,
    ranks_hbm, routes_hbm, owner_hbm, boundary_hbm, left_hbm, right_hbm, weight_hbm,
    bound_out, env_out,
    ranks, routes, owner, boundary, left, right, weight, in_sem,
    left_bf, left_in, right_bf, product, chain_in, pairs, starts, prefixes, moved, terms, info, chosen,
    left_send, left_recv, chain_send, chain_recv, pair_send, pair_recv,
    start_send, start_recv, start_twin, prefix_send, prefix_recv, prefix_twin, info_send, info_recv,
):
    row, sector = lax.axis_index("row"), lax.axis_index("sector")
    slots = weight.shape[1]
    block, width = boundary.shape[1], boundary.shape[2]
    piece_rows = width // slices
    piece = lax.rem(sector, slices)
    group_base = sector - piece
    groups = sectors // 2
    group, core = sector // 2, lax.rem(sector, 2)
    twin = group * 2 + 1 - core

    barrier = pltpu.get_barrier_semaphore()
    for step in range(1, rows):
        pl.semaphore_signal(barrier, inc=1, device_id=(lax.rem(row + step, rows), sector), device_id_type=MESH)
    for step in range(1, sectors):
        pl.semaphore_signal(barrier, inc=1, device_id=(row, lax.rem(sector + step, sectors)), device_id_type=MESH)

    loads = [
        pltpu.make_async_copy(source, target, in_sem.at[at])
        for at, (source, target) in enumerate((
            (right_hbm, right), (left_hbm, left), (boundary_hbm, boundary), (ranks_hbm, ranks),
            (routes_hbm, routes), (owner_hbm, owner), (weight_hbm, weight)))
    ]
    for load in loads:
        load.start()
    loads[0].wait()
    right_bf[...] = right[0].astype(BF16)
    loads[1].wait()
    left_bf[...] = left[0, 0].astype(BF16)
    loads[2].wait()
    starts[sector] = boundary[0].astype(BF16)
    for load in loads[3:6]:
        load.wait()
    for j in range(slots):
        info[sector, pl.ds(j, 1), :] = jnp.full((1, 128), owner[routes[0, j]], jnp.int32).astype(F32)

    @pl.when(row == 0)
    def _():
        masked = jnp.where(lax.broadcasted_iota(jnp.int32, (block, width), 0) < ranks[0], boundary[0], 0.0)
        change = jnp.dot(left_bf[...], masked.astype(BF16), preferred_element_type=F32)
        full = jnp.where(
            lax.broadcasted_iota(jnp.int32, (block, width), 0) < ranks[0], 0.9 * masked + change, 0.0)
        starts[sector] = full.astype(BF16)
        at = lax.broadcasted_iota(jnp.int32, (piece_rows, width), 0) + piece * piece_rows
        unit = at == lax.broadcasted_iota(jnp.int32, (piece_rows, width), 1)
        chain_in[...] = jnp.where(unit, 1.0, 0.0).astype(BF16)

    pl.semaphore_wait(barrier, rows - 1 + sectors - 1)

    def chain_copy():
        return pltpu.make_async_remote_copy(
            src_ref=pairs.at[piece], dst_ref=chain_in, send_sem=chain_send, recv_sem=chain_recv,
            device_id=(lax.rem(row + 1, rows), sector), device_id_type=MESH)

    def left_copy(slot, target):
        return pltpu.make_async_remote_copy(
            src_ref=left_bf, dst_ref=left_in.at[slot], send_sem=left_send.at[target], recv_sem=left_recv.at[slot],
            device_id=(target, sector), device_id_type=MESH)

    def in_plane(buffer, slot, send_sem, recv_sem, target):
        return pltpu.make_async_remote_copy(
            src_ref=buffer.at[slot], dst_ref=buffer.at[slot], send_sem=send_sem, recv_sem=recv_sem.at[slot],
            device_id=(row, target), device_id_type=MESH)

    def info_copy(slot, step, target):
        return in_plane(info, slot, info_send.at[step], info_recv, target)

    def pair_copy(slot, step, target):
        return in_plane(pairs, slot, pair_send.at[step], pair_recv, target)

    def start_copy(slot, sem, target):
        return in_plane(starts, slot, sem, start_recv, target)

    def prefix_copy(slot, sem, target):
        return in_plane(prefixes, slot, sem, prefix_recv, target)

    def chain_step():
        @pl.when(row > 0)
        def _():
            chain_copy().wait_recv()
        before = chain_in[...]
        after = 0.9 * before.astype(F32) + jnp.dot(before, right_bf[...], preferred_element_type=F32)
        pairs[piece] = after.astype(BF16)

        @pl.when(row < rows - 1)
        def _():
            chain_copy().start()

    def pair_step():
        for step in range(1, slices):
            pair_copy(piece, step, group_base + partner(piece, step, slices)[0]).start()

    pl.when(row == 0)(chain_step)

    for target in range(rows - 1, 0, -1):
        @pl.when(row < target)
        def _():
            left_copy(row, target).start()
    for step in range(1, sectors):
        info_copy(sector, step, lax.rem(sector + step, sectors)).start()
    pl.when(row == 0)(pair_step)
    for step in range(groups - 1, 0, -1):
        start_copy(sector, start_send.at[step], partner(group, step, groups)[0] * 2 + core).start()
    start_copy(sector, start_send.at[0], twin).start()

    @pl.when((row > 0) & (row < rows - 1))
    def _():
        chain_step()
        pair_step()

    loads[6].wait()
    for step in range(1, sectors):
        source = lax.rem(sector + step, sectors)
        info_copy(source, step, source).wait_recv()
    me = sector.astype(F32)
    for source in range(sectors):
        picked = jnp.zeros((width, width), BF16)
        for j in range(slots):
            mark = info[source, pl.ds(j, 1), :]
            mark = jnp.concatenate([mark] * (width // 128), axis=1)
            same = jnp.where(mark == me, 1.0, 0.0).astype(BF16)
            picked = picked + weight[0, j] * same
        chosen[source] = picked

    across = lax.broadcasted_iota(jnp.int32, (block, block), 1)
    down = lax.broadcasted_iota(jnp.int32, (block, block), 0)
    kept = across < ranks[0]
    own = jnp.where(across == down, 0.9, 0.0) + left[0, 0]
    product[...] = jnp.where(kept & (down < ranks[0]), own, 0.0)
    for source in range(rows - 2, -1, -1):
        @pl.when(source < row)
        def _():
            left_copy(source, source + 1).wait_recv()
            value = product[...]
            change = jnp.dot(value.astype(BF16), left_in[source], preferred_element_type=F32)
            product[...] = jnp.where(kept, 0.9 * value + change, 0.0)
    prefixes[sector] = product[...].astype(BF16)

    @pl.when(row > 0)
    def _():
        for step in range(groups - 1, 0, -1):
            prefix_copy(sector, prefix_send.at[step], partner(group, step, groups)[0] * 2 + core).start()
        prefix_copy(sector, prefix_send.at[0], twin).start()

    @pl.when((row > 0) & (row == rows - 1))
    def _():
        chain_step()
        pair_step()

    for step in range(groups - 1, 0, -1):
        slot = partner(group, step, groups)[1] * 2 + core
        start_copy(slot, start_send.at[step], slot).wait_recv()
        start_copy(slot, start_twin.at[step], twin).start()

    @pl.when(row > 0)
    def _():
        for step in range(groups - 1, 0, -1):
            slot = partner(group, step, groups)[1] * 2 + core
            prefix_copy(slot, prefix_send.at[step], slot).wait_recv()
            prefix_copy(slot, prefix_twin.at[step], twin).start()

    start_copy(twin, start_send.at[0], twin).wait_recv()
    for step in range(groups - 1, 0, -1):
        start_copy(partner(group, step, groups)[1] * 2 + 1 - core, start_twin.at[step], twin).wait_recv()
    for step in range(1, slices):
        slot = partner(piece, step, slices)[1]
        pair_copy(slot, step, group_base + slot).wait_recv()
    all_pairs = pairs[...].reshape(width, width)
    for source in range(sectors):
        moved[source] = jnp.dot(starts[source], all_pairs, preferred_element_type=F32).astype(BF16)
    for source in range(sectors):
        terms[source] = jnp.dot(moved[source], chosen[source], preferred_element_type=F32).astype(BF16)

    @pl.when(row == 0)
    def _():
        bound_out[0, 0] = jnp.dot(starts[sector], all_pairs, preferred_element_type=F32)
        total = terms[0].astype(F32)
        for source in range(1, sectors):
            total = total + terms[source].astype(F32)
        env_out[0, 0] = total

    @pl.when(row > 0)
    def _():
        bound_out[0, 0] = jnp.dot(prefixes[sector], moved[sector], preferred_element_type=F32)
        prefix_copy(twin, prefix_send.at[0], twin).wait_recv()
        for step in range(groups - 1, 0, -1):
            prefix_copy(partner(group, step, groups)[1] * 2 + 1 - core, prefix_twin.at[step], twin).wait_recv()
        total = jnp.zeros((block, width), F32)
        for first in range(0, sectors, 2):
            both = jnp.concatenate([prefixes[first], prefixes[first + 1]], axis=1)
            total = total + jnp.dot(
                both, terms[pl.ds(first, 2)].reshape(2 * block, width), preferred_element_type=F32)
        env_out[0, 0] = total

    for target in range(1, rows):
        @pl.when(row < target)
        def _():
            left_copy(row, target).wait_send()

    @pl.when(row < rows - 1)
    def _():
        chain_copy().wait_send()
    for step in range(1, sectors):
        info_copy(sector, step, lax.rem(sector + step, sectors)).wait_send()
    for step in range(1, slices):
        pair_copy(piece, step, group_base + partner(piece, step, slices)[0]).wait_send()

    def all_left(copy, first, second):
        copy(sector, first.at[0], twin).wait_send()
        for step in range(1, groups):
            to, source = partner(group, step, groups)
            copy(sector, first.at[step], to * 2 + core).wait_send()
            copy(source * 2 + core, second.at[step], twin).wait_send()

    all_left(start_copy, start_send, start_twin)
    pl.when(row > 0)(functools.partial(all_left, prefix_copy, prefix_send, prefix_twin))


def solution(mesh):
    rows, sectors = mesh.shape["row"], mesh.shape["sector"]

    def on_device(boundary_in, left, right, weight, ranks, routes, owner):
        block, width = boundary_in.shape[1:]
        slots = weight.shape[1]
        slices = min(sectors, width // 16)
        out = pltpu.VMEM((1, 1, block, width), F32)
        vmem = pl.BlockSpec(memory_space=pltpu.VMEM)
        dma = pltpu.SemaphoreType.DMA
        operands = (ranks, routes, owner, boundary_in, left, right, weight)
        return pl.pallas_call(
            functools.partial(kernel, rows, sectors, slices),
            out_shape=(out, out),
            in_specs=[pl.BlockSpec(memory_space=pltpu.HBM)] * len(operands),
            out_specs=(vmem, vmem),
            scratch_shapes=[
                *(pltpu.SMEM(operand.shape, operand.dtype) for operand in operands[:3]),
                *(pltpu.VMEM(operand.shape, operand.dtype) for operand in operands[3:]),
                dma((len(operands),)),
                pltpu.VMEM((block, block), BF16),
                pltpu.VMEM((rows - 1, block, block), BF16),
                pltpu.VMEM((width, width), BF16),
                pltpu.VMEM((block, block), F32),
                pltpu.VMEM((width // slices, width), BF16),
                pltpu.VMEM((slices, width // slices, width), BF16),
                pltpu.VMEM((sectors, block, width), BF16),
                pltpu.VMEM((sectors, block, block), BF16),
                pltpu.VMEM((sectors, block, width), BF16),
                pltpu.VMEM((sectors, block, width), BF16),
                pltpu.VMEM((sectors, max(8, slots), 128), F32),
                pltpu.VMEM((sectors, width, width), BF16),
                dma((rows,)), dma((rows,)), dma, dma, dma((slices,)), dma((slices,)),
                dma((sectors // 2,)), dma((sectors,)), dma((sectors // 2,)),
                dma((sectors // 2,)), dma((sectors,)), dma((sectors // 2,)),
                dma((sectors,)), dma((sectors,)),
            ],
            compiler_params=pltpu.CompilerParams(
                collective_id=0, has_side_effects=True, vmem_limit_bytes=60 * 2**20),
        )(*operands)

    return jax.shard_map(
        on_device,
        mesh=mesh,
        in_specs=(
            P("sector", None, None),
            P("row", "sector", None, None),
            P("row", None, None),
            P("row", None, None, None),
            P("sector"),
            P("sector", None),
            P(),
        ),
        out_specs=(P("row", "sector", None, None), P("row", "sector", None, None)),
        check_vma=False,
    )
```
